256 devices in a mesh: dp: 32 (over y_lo, z, core), mp: 8 (over y_hi, x).
Axes of the slice: x: 4, y: 4 (y_hi: 2, y_lo: 2; y = y_hi * 2 + y_lo), z: 8, core: 2. Of those that a mesh axis runs over, the one named last changes fastest.
Arguments:
- normed: bfloat16 [4096, 6144], P('dp', 'mp'), may hold values from -6 to 6
- cotangent: bfloat16 [4096, 6144], P('dp', 'mp'), may hold values from -6 to 6
- up_weight: bfloat16 [6144, 12288], P('mp', 'dp'), may hold values from -0.078125 to 0.078125
- up_probe: bfloat16 [6144, 12288], P('mp', 'dp'), may hold values from -5 to 5
- down_weight: bfloat16 [6144, 12288], P('mp', 'dp'), may hold values from -0.0546875 to 0.0546875
Outputs:
- up_grad: bfloat16 [6144, 12288], P('mp', 'dp')
- up_estimate: bfloat16 [6144, 12288], P('mp', 'dp')
The draws below stay inside these ranges and needn't reach their ends.
All inputs are finite; a program needn't handle non-finite values.
Results may differ from the reference program's by a relative error of at most 0.0049.
Values may be sent and summed in bfloat16 or wider, within the bound.
A program may use at most 128 MiB of HBM per device.

```python
import math
import jax
import jax.numpy as jnp

D = 6144
FF = 12288
TOKENS = 4096


def raised(array, rng, source, target, shards_of, factor):
    owner, partner = [(jnp.arange(array.shape[dim]) // (array.shape[dim] // shards_of)).reshape([-1 if axis == dim else 1 for axis in range(array.ndim)]) for dim in (source, target)]
    chosen = jax.random.permutation(rng, shards_of)[partner]
    strong = (owner == chosen) | (owner == (partner + shards_of // 2) % shards_of)
    return jnp.where(strong, factor * array, array)


def shard_levels(own_key, shape, cuts, least, largest):
    level = 1.0
    for position, shards_of in cuts:
        heights = jax.random.uniform(jax.random.fold_in(jax.random.fold_in(own_key, 6), position), (shards_of,), jnp.float32, least / len(cuts), largest / len(cuts))
        level = level * jnp.repeat(jnp.exp(heights), shape[position] // shards_of).reshape((-1,) + (1,) * (len(shape) - 1 - position))
    return level


def noise(rng, extent, width, reach, cuts=(), held_as=jnp.bfloat16):
    values = width * jax.random.normal(rng, extent, jnp.float32)
    if cuts:
        values = values * shard_levels(rng, extent, cuts, -0.22, 0.18)
    return jnp.clip(values, -reach, reach).astype(held_as)


def gaussian_with(stream_key, extent, width, limit, shards, heavy, held_as=jnp.bfloat16):
    entries = width * jax.random.normal(stream_key, extent, jnp.float32)
    if shards:
        entries = entries * shard_levels(stream_key, extent, shards, -0.22, 0.18)
    return jnp.clip(raised(entries, jax.random.fold_in(stream_key, 3), *heavy), -limit, limit).astype(held_as)


def setup_inputs(seed: int = 0) -> dict:
    keys = jax.random.split(jax.random.key(seed), 6)
    return {
        "normed": gaussian_with(keys[0], (TOKENS, D), 1.0, 6.0, ((0, 32), (1, 8)), (1, 0, 32, 2.75)),
        "cotangent": noise(keys[1], (TOKENS, D), 1.0, 6.0, ((0, 32), (1, 8))),
        "up_weight": noise(keys[2], (D, FF), D ** -0.5, 0.078125, ((0, 8), (1, 32))),
        "up_probe": noise(keys[3], (D, FF), 1.0, 5.0, ((0, 8), (1, 32))),
        "down_weight": noise(keys[4], (D, FF), FF ** -0.5, 0.0546875, ((0, 8), (1, 32))),
    }


def curvature_terms(preact, preact_dot, upstream):
    density = jnp.exp(-0.5 * preact * preact) / math.sqrt(2.0 * math.pi)
    cumulative = 0.5 * (1.0 + jax.scipy.special.erf(preact / math.sqrt(2.0)))
    slope = cumulative + preact * density
    bend = density * (2.0 - preact * preact)
    delta = (upstream * slope).astype(jnp.bfloat16)
    delta_dot = (upstream * bend * preact_dot).astype(jnp.bfloat16)
    return (delta, delta_dot)

def reference(normed, cotangent, up_weight, up_probe, down_weight):
    preact = jnp.dot(normed, up_weight, preferred_element_type=jnp.float32)
    preact_dot = jnp.dot(normed, up_probe, preferred_element_type=jnp.float32)
    upstream = jnp.dot(cotangent, down_weight, preferred_element_type=jnp.float32)
    delta, delta_dot = curvature_terms(preact, preact_dot, upstream)
    inverse = 1.0 / float(TOKENS)
    up_sum = jnp.dot(normed.T, delta, preferred_element_type=jnp.float32)
    up_curv = jnp.dot(normed.T, delta_dot, preferred_element_type=jnp.float32)
    up_grad = (up_sum * inverse).astype(jnp.bfloat16)
    up_estimate = (up_probe.astype(jnp.float32) * (up_curv * inverse)).astype(jnp.bfloat16)
    return (up_grad, up_estimate)
```

```python
import math

import jax
import jax.numpy as jnp
from jax import lax
from jax.experimental import pallas as pl
from jax.experimental.pallas import tpu as pltpu
from jax.sharding import PartitionSpec as P

MESH = pl.DeviceIdType.MESH
TOKENS = 4096
BLOCK = 768
CHUNK = 128
NF = 3
ITEMS = 24
LAG_A, LAG_B = 2, 4


def curvature_terms(preact, preact_dot, upstream):
    density = jnp.exp(-0.5 * preact * preact) / math.sqrt(2.0 * math.pi)
    cumulative = 0.5 * (1.0 + lax.erf(preact / math.sqrt(2.0)))
    slope = cumulative + preact * density
    bend = density * (2.0 - preact * preact)
    delta = (upstream * slope).astype(jnp.bfloat16)
    delta_dot = (upstream * bend * preact_dot).astype(jnp.bfloat16)
    return delta, delta_dot


def dot(a, b):
    return jnp.dot(a, b, preferred_element_type=jnp.float32)


def dot_t(a, b):
    return lax.dot_general(a, b, (((0,), (0,)), ((), ())), preferred_element_type=jnp.float32)


def item(i):
    f = jnp.where(i < 6, i // 3, jnp.where(i < 10, (i - 6) // 2, jnp.where(i < 15, 2, (i - 15) // 3)))
    j = jnp.where(i < 6, i % 3, jnp.where(i < 10, 3 + (i - 6) % 2, jnp.where(i < 15, i - 10, 5 + (i - 15) % 3)))
    return f, j


def kernel(normed, cotangent, up_weight, up_probe, down_weight, grad, est,
           abuf, wbuf, pbuf, ptmp, rbuf, dbuf, acc, osend, orecv,
           la, lw, ysend, yrecv, zsend, zrecv, csend, crecv, wsend, wrecv,
           rsend, rrecv, gsend, grecv, osem, orsem):
    dp, mp = lax.axis_index("dp"), lax.axis_index("mp")
    l, z, c = dp // 16, (dp // 2) % 8, dp % 2
    h, x = mp // 4, mp % 4

    def at(x_=x, h_=h, l_=l, z_=z, c_=c):
        return (l_ * 16 + z_ * 2 + c_, h_ * 4 + x_)

    def wait(ref, sem):
        pltpu.make_async_copy(ref, ref, sem).wait()

    def send(src, dst, ssem, rsem, device):
        pltpu.make_async_remote_copy(src_ref=src, dst_ref=dst, send_sem=ssem, recv_sem=rsem,
                                     device_id=device, device_id_type=MESH).start()

    x_peers = [at(x_=(x + dx) % 4) for dx in (1, 2, 3)]
    y_peers = [at(l_=1 - l), at(l_=1 - l, h_=1 - h), at(h_=1 - h)]
    z_peers = [at(z_=(z + 1) % 8), at(z_=(z + 7) % 8)]
    sibling = at(c_=1 - c)
    partner = at(h_=1 - h)

    def rows_of(cc, ll):
        return pl.ds(pl.multiple_of(cc * 128 + ll * 64, 64), 64)

    mine = pl.ds(pl.multiple_of(h * 64, 64), 64)
    theirs = pl.ds(pl.multiple_of((1 - h) * 64, 64), 64)
    inputs = (normed, cotangent)
    for n in range(2):
        pltpu.make_async_copy(inputs[n].at[mine, :], abuf.at[n, h, z, rows_of(c, l), :], la).start()
    for f in range(NF):
        for k, w in enumerate((up_weight, up_probe, down_weight)):
            pltpu.make_async_copy(w.at[:, pl.ds(f * CHUNK, CHUNK)],
                                  wbuf.at[f, h, :, pl.ds(k * CHUNK, CHUNK)], lw.at[f]).start()

    barrier = pltpu.get_barrier_semaphore()
    peers = x_peers + y_peers + z_peers + [sibling]
    for peer in peers:
        pl.semaphore_signal(barrier, inc=1, device_id=peer, device_id_type=MESH)
    pl.semaphore_wait(barrier, len(peers))

    def region(zz, cc, s):
        ll = (l + (s + 1) // 2) % 2
        hh = (h + s // 2) % 2
        return abuf.at[:, hh, zz, rows_of(cc, ll), :]

    def zpart(way, k):
        return (k % 4 + 2 * (k // 12)) % 4 if way else k % 4

    def ring_send(way, k):
        sign = -1 if way else 1
        zz = (z + 8 - sign * (k // 4)) % 8
        r = region(zz, c, zpart(way, k))
        send(r, r, zsend.at[way], zrecv.at[way, k], z_peers[way])

    def core_send(zz, s):
        r = region(zz, c, s)
        send(r, r, csend, crecv.at[zz], sibling)

    def core_wait(zz):
        wait(abuf.at[:, :, zz, pl.ds(pl.multiple_of((1 - c) * 128, 128), 128), :], crecv.at[zz])

    for s in (1, 2, 3):
        for n in range(2):
            send(inputs[n].at[mine if s == 1 else theirs, :], abuf.at[n, h, z, rows_of(c, l), :],
                 ysend.at[s - 1], yrecv.at[s - 1], y_peers[s - 1])

    def weight_send(f):
        wait(wbuf.at[f, h], lw.at[f])
        send(wbuf.at[f, h], wbuf.at[f, h], wsend, wrecv.at[f], partner)

    wait(region(z, c, 0), la)
    ring_send(0, 0)
    ring_send(1, 0)
    core_send(z, 0)
    weight_send(0)
    acc[...] = jnp.zeros_like(acc)
    for s in (1, 2, 3):
        wait(region(z, c, s), yrecv.at[s - 1])
        ring_send(0, s)
        ring_send(1, s)
        core_send(z, s)
    core_wait(z)

    def tick(k):
        for way in (0, 1):
            sign = -1 if way else 1
            zz = (z + 8 - sign * (k // 4 + 1)) % 8
            s = zpart(way, k)
            wait(region(zz, c, s), zrecv.at[way, k])
            if way == 0:
                @pl.when(k <= 9)
                def _():
                    ring_send(0, k + 4)
            else:
                @pl.when(k <= 7)
                def _():
                    ring_send(1, k + 4)

                @pl.when((k == 10) | (k == 11))
                def _():
                    ring_send(1, k + 2)
            core_send(zz, s)

        @pl.when((k < 12) & (k % 4 == 3))
        def _():
            core_wait((z + k // 4 + 1) % 8)
            core_wait((z + 7 - k // 4) % 8)

        @pl.when(k == 13)
        def _():
            core_wait((z + 4) % 8)

    def early(k, carry):
        tick(k)

        @pl.when(k == 2)
        def _():
            weight_send(1)
        return carry

    lax.fori_loop(0, 4, early, 0)

    def packet(j):
        return (z + 8 + (2 * (j % 2) - 1) * ((j + 1) // 2)) % 8

    def x_rows(xx):
        return pl.ds(pl.multiple_of(xx * 64, 64), 64)

    def forward(i):
        f, j = item(i)
        zj = packet(j)
        slot = i % 4
        for n, cols in ((0, pl.ds(0, 2 * CHUNK)), (1, pl.ds(2 * CHUNK, CHUNK))):
            part = dot(abuf[n, 0, zj], wbuf[f, 0, :, cols]) + dot(abuf[n, 1, zj], wbuf[f, 1, :, cols])
            ptmp[slot, :, cols] = part
            pbuf[f, zj, :, cols] = part.astype(jnp.bfloat16)
        for dx in (1, 2, 3):
            send(pbuf.at[f, zj, x_rows((x + dx) % 4), :], rbuf.at[f, zj, dx - 1],
                 rsend, rrecv.at[f, zj], x_peers[dx - 1])

    def terms(i):
        f, j = item(i)
        zj = packet(j)
        slot = i % 4
        wait(rbuf.at[f, zj], rrecv.at[f, zj])

        def total(k):
            cols = pl.ds(k * CHUNK, CHUNK)
            t = ptmp[slot, x_rows(x), cols]
            for s in range(3):
                t = t + rbuf[f, zj, s, :, cols].astype(jnp.float32)
            return t

        delta, delta_dot = curvature_terms(total(0), total(1), total(2))
        dbuf[f, zj, x_rows(x), pl.ds(0, CHUNK)] = delta
        dbuf[f, zj, x_rows(x), pl.ds(CHUNK, CHUNK)] = delta_dot
        r = dbuf.at[f, zj, x_rows(x), :]
        for dx in (1, 2, 3):
            send(r, r, gsend, grecv.at[f, zj], x_peers[dx - 1])

    def backward(i):
        f, j = item(i)
        zj = packet(j)
        wait(dbuf.at[f, zj, pl.ds(0, 192), :], grecv.at[f, zj])
        d = dbuf[f, zj]
        for hh in range(2):
            acc[f, hh] += dot_t(abuf[0, hh, zj], d)

    def out_send(f):
        osend[f] = acc[f, 1 - h].astype(jnp.bfloat16)
        send(osend.at[f], orecv.at[f], osem, orsem.at[f], partner)

    def step(i, carry):
        @pl.when(i < 10)
        def _():
            tick(i + 4)

        @pl.when(i == 0)
        def _():
            wait(wbuf.at[0, 1 - h], wrecv.at[0])
            weight_send(2)

        @pl.when(i == 3)
        def _():
            wait(wbuf.at[1, 1 - h], wrecv.at[1])

        @pl.when(i == 10)
        def _():
            wait(wbuf.at[2, 1 - h], wrecv.at[2])

        @pl.when(i < ITEMS)
        def _():
            forward(i)

        @pl.when((i >= LAG_A) & (i < ITEMS + LAG_A))
        def _():
            terms(i - LAG_A)

        @pl.when(i >= LAG_B)
        def _():
            backward(i - LAG_B)

        done = i - LAG_B

        @pl.when((done >= 15) & (done % 3 == 2))
        def _():
            out_send((done - 15) // 3)
        return carry

    lax.fori_loop(0, ITEMS + LAG_B, step, 0)

    inverse = 1.0 / float(TOKENS)
    for f in range(NF):
        wait(orecv.at[f], orsem.at[f])
        cols = pl.ds(f * CHUNK, CHUNK)
        g = acc[f, h, :, pl.ds(0, CHUNK)] + orecv[f, :, pl.ds(0, CHUNK)].astype(jnp.float32)
        grad[:, cols] = (g * inverse).astype(jnp.bfloat16)
        e = acc[f, h, :, pl.ds(CHUNK, CHUNK)] + orecv[f, :, pl.ds(CHUNK, CHUNK)].astype(jnp.float32)
        probe = wbuf[f, h, :, pl.ds(CHUNK, CHUNK)].astype(jnp.float32)
        est[:, cols] = (probe * (e * inverse)).astype(jnp.bfloat16)

    for s in range(3):
        wait(region(z, c, 0), ysend.at[s])
    for way in range(2):
        wait(abuf.at[:, 0, pl.ds(0, 7), pl.ds(0, 128), :], zsend.at[way])
    wait(abuf.at[:, :, :, pl.ds(0, 128), :], csend)
    wait(wbuf.at[:, 0], wsend)
    wait(rbuf, rsend)
    wait(dbuf.at[:, :, pl.ds(0, 192), :], gsend)
    wait(osend, osem)


def per_device(*args):
    bf, f32 = jnp.bfloat16, jnp.float32
    dma = pltpu.SemaphoreType.DMA
    hidden = args[2].shape[1]
    return pl.pallas_call(
        kernel,
        out_shape=[jax.ShapeDtypeStruct((BLOCK, hidden), bf)] * 2,
        in_specs=[pl.BlockSpec(memory_space=pl.ANY)] * 5,
        out_specs=[pl.BlockSpec(memory_space=pltpu.VMEM)] * 2,
        scratch_shapes=[
            pltpu.VMEM((2, 2, 8, 256, BLOCK), bf),
            pltpu.VMEM((NF, 2, BLOCK, 3 * CHUNK), bf),
            pltpu.VMEM((NF, 8, 256, 3 * CHUNK), bf),
            pltpu.VMEM((4, 256, 3 * CHUNK), f32),
            pltpu.VMEM((NF, 8, 3, 64, 3 * CHUNK), bf),
            pltpu.VMEM((NF, 8, 256, 2 * CHUNK), bf),
            pltpu.VMEM((NF, 2, BLOCK, 2 * CHUNK), f32),
            pltpu.VMEM((NF, BLOCK, 2 * CHUNK), bf),
            pltpu.VMEM((NF, BLOCK, 2 * CHUNK), bf),
            dma, dma((NF,)),
            dma((3,)), dma((3,)),
            dma((2,)), dma((2, 14)),
            dma, dma((8,)),
            dma, dma((NF,)),
            dma, dma((NF, 8)),
            dma, dma((NF, 8)),
            dma, dma((NF,)),
        ],
        compiler_params=pltpu.CompilerParams(
            collective_id=0, has_side_effects=True, vmem_limit_bytes=56 * 2**20
        ),
        cost_estimate=pl.CostEstimate(flops=12 * 10**9, bytes_accessed=4 * 10**6, transcendentals=10**6),
    )(*args)


def solution(mesh):
    placed = (P("dp", "mp"), P("dp", "mp"), P("mp", "dp"), P("mp", "dp"), P("mp", "dp"))
    return jax.shard_map(
        per_device,
        mesh=mesh,
        in_specs=placed,
        out_specs=(P("mp", "dp"), P("mp", "dp")),
        check_vma=False,
    )
```

```python
import math

import jax
import jax.numpy as jnp
from jax import lax
from jax.experimental import pallas as pl
from jax.experimental.pallas import tpu as pltpu
from jax.sharding import PartitionSpec as P

MESH = pl.DeviceIdType.MESH
TOKENS = 4096
BLOCK = 768
CHUNK = 128
NF = 3
ITEMS = 24
LAG_A, LAG_B = 2, 4


def curvature_terms(preact, preact_dot, upstream):
    density = jnp.exp(-0.5 * preact * preact) / math.sqrt(2.0 * math.pi)
    cumulative = 0.5 * (1.0 + lax.erf(preact / math.sqrt(2.0)))
    slope = cumulative + preact * density
    bend = density * (2.0 - preact * preact)
    delta = (upstream * slope).astype(jnp.bfloat16)
    delta_dot = (upstream * bend * preact_dot).astype(jnp.bfloat16)
    return delta, delta_dot


def dot(a, b):
    return jnp.dot(a, b, preferred_element_type=jnp.float32)


def dot_t(a, b):
    return lax.dot_general(a, b, (((0,), (0,)), ((), ())), preferred_element_type=jnp.float32)


def item(i):
    f = jnp.where(i < 6, i // 3, jnp.where(i < 10, (i - 6) // 2, jnp.where(i < 15, 2, (i - 15) // 3)))
    j = jnp.where(i < 6, i % 3, jnp.where(i < 10, 3 + (i - 6) % 2, jnp.where(i < 15, i - 10, 5 + (i - 15) % 3)))
    return f, j


def kernel(normed, cotangent, up_weight, up_probe, down_weight, grad, est,
           abuf, wbuf, pbuf, ptmp, rbuf, dbuf, acc, osend, orecv,
           la, lw, ysend, yrecv, zsend, zrecv, csend, crecv, wsend, wrecv,
           rsend, rrecv, gsend, grecv, osem, orsem):
    dp, mp = lax.axis_index("dp"), lax.axis_index("mp")
    l, z, c = dp // 16, (dp // 2) % 8, dp % 2
    h, x = mp // 4, mp % 4

    def at(x_=x, h_=h, l_=l, z_=z, c_=c):
        return (l_ * 16 + z_ * 2 + c_, h_ * 4 + x_)

    def wait(ref, sem):
        pltpu.make_async_copy(ref, ref, sem).wait()

    def send(src, dst, ssem, rsem, device):
        pltpu.make_async_remote_copy(src_ref=src, dst_ref=dst, send_sem=ssem, recv_sem=rsem,
                                     device_id=device, device_id_type=MESH).start()

    x_peers = [at(x_=(x + dx) % 4) for dx in (1, 2, 3)]
    y_peers = [at(l_=1 - l), at(l_=1 - l, h_=1 - h), at(h_=1 - h)]
    z_peers = [at(z_=(z + 1) % 8), at(z_=(z + 7) % 8)]
    sibling = at(c_=1 - c)
    partner = at(h_=1 - h)

    def rows_of(cc, ll):
        return pl.ds(pl.multiple_of(cc * 128 + ll * 64, 64), 64)

    mine = pl.ds(pl.multiple_of(h * 64, 64), 64)
    theirs = pl.ds(pl.multiple_of((1 - h) * 64, 64), 64)
    inputs = (normed, cotangent)
    for n in range(2):
        pltpu.make_async_copy(inputs[n].at[mine, :], abuf.at[n, h, z, rows_of(c, l), :], la).start()
    for f in range(NF):
        for k, w in enumerate((up_weight, up_probe, down_weight)):
            pltpu.make_async_copy(w.at[:, pl.ds(f * CHUNK, CHUNK)],
                                  wbuf.at[f, h, :, pl.ds(k * CHUNK, CHUNK)], lw.at[f]).start()

    barrier = pltpu.get_barrier_semaphore()
    peers = x_peers + y_peers + z_peers + [sibling]
    for peer in peers:
        pl.semaphore_signal(barrier, inc=1, device_id=peer, device_id_type=MESH)
    pl.semaphore_wait(barrier, len(peers))

    def region(zz, cc, s):
        ll = (l + (s + 1) // 2) % 2
        hh = (h + s // 2) % 2
        return abuf.at[:, hh, zz, rows_of(cc, ll), :]

    def zpart(way, k):
        return (k % 4 + 2 * (k // 12)) % 4 if way else k % 4

    def ring_send(way, k):
        sign = -1 if way else 1
        zz = (z + 8 - sign * (k // 4)) % 8
        r = region(zz, c, zpart(way, k))
        send(r, r, zsend.at[way], zrecv.at[way, k], z_peers[way])

    def core_send(zz, s):
        r = region(zz, c, s)
        send(r, r, csend, crecv.at[zz], sibling)

    def core_wait(zz):
        wait(abuf.at[:, :, zz, pl.ds(pl.multiple_of((1 - c) * 128, 128), 128), :], crecv.at[zz])

    for s in (1, 2, 3):
        for n in range(2):
            send(inputs[n].at[mine if s == 1 else theirs, :], abuf.at[n, h, z, rows_of(c, l), :],
                 ysend.at[s - 1], yrecv.at[s - 1], y_peers[s - 1])

    def weight_send(f):
        wait(wbuf.at[f, h], lw.at[f])
        send(wbuf.at[f, h], wbuf.at[f, h], wsend, wrecv.at[f], partner)

    wait(region(z, c, 0), la)
    ring_send(0, 0)
    ring_send(1, 0)
    core_send(z, 0)
    acc[...] = jnp.zeros_like(acc)
    for s in (1, 2, 3):
        if s == 3:
            weight_send(0)
        wait(region(z, c, s), yrecv.at[s - 1])
        ring_send(0, s)
        ring_send(1, s)
        core_send(z, s)

    def tick(k):
        for way in (0, 1):
            sign = -1 if way else 1
            zz = (z + 8 - sign * (k // 4 + 1)) % 8
            s = zpart(way, k)
            wait(region(zz, c, s), zrecv.at[way, k])
            if way == 0:
                @pl.when(k <= 9)
                def _():
                    ring_send(0, k + 4)
            else:
                @pl.when(k <= 7)
                def _():
                    ring_send(1, k + 4)

                @pl.when((k == 10) | (k == 11))
                def _():
                    ring_send(1, k + 2)
            core_send(zz, s)

    def early(k, carry):
        tick(k)

        @pl.when(k == 2)
        def _():
            weight_send(1)
        return carry

    lax.fori_loop(0, 3, early, 0)

    def packet(j):
        return (z + 8 + (2 * (j % 2) - 1) * ((j + 1) // 2)) % 8

    def x_rows(xx):
        return pl.ds(pl.multiple_of(xx * 64, 64), 64)

    def forward(i):
        f, j = item(i)
        zj = packet(j)
        slot = i % 4
        for n, cols in ((0, pl.ds(0, 2 * CHUNK)), (1, pl.ds(2 * CHUNK, CHUNK))):
            part = dot(abuf[n, 0, zj], wbuf[f, 0, :, cols]) + dot(abuf[n, 1, zj], wbuf[f, 1, :, cols])
            ptmp[slot, :, cols] = part
            pbuf[f, zj, :, cols] = part.astype(jnp.bfloat16)
        for dx in (1, 2, 3):
            send(pbuf.at[f, zj, x_rows((x + dx) % 4), :], rbuf.at[f, zj, dx - 1],
                 rsend, rrecv.at[f, zj], x_peers[dx - 1])

    def terms(i):
        f, j = item(i)
        zj = packet(j)
        slot = i % 4
        wait(rbuf.at[f, zj], rrecv.at[f, zj])

        def total(k):
            cols = pl.ds(k * CHUNK, CHUNK)
            t = ptmp[slot, x_rows(x), cols]
            for s in range(3):
                t = t + rbuf[f, zj, s, :, cols].astype(jnp.float32)
            return t

        delta, delta_dot = curvature_terms(total(0), total(1), total(2))
        dbuf[f, zj, x_rows(x), pl.ds(0, CHUNK)] = delta
        dbuf[f, zj, x_rows(x), pl.ds(CHUNK, CHUNK)] = delta_dot
        r = dbuf.at[f, zj, x_rows(x), :]
        for dx in (1, 2, 3):
            send(r, r, gsend, grecv.at[f, zj], x_peers[dx - 1])

    def backward(i):
        f, j = item(i)
        zj = packet(j)
        wait(dbuf.at[f, zj, pl.ds(0, 192), :], grecv.at[f, zj])
        d = dbuf[f, zj]
        for hh in range(2):
            acc[f, hh] += dot_t(abuf[0, hh, zj], d)

    def out_send(f):
        osend[f] = acc[f, 1 - h].astype(jnp.bfloat16)
        send(osend.at[f], orecv.at[f], osem, orsem.at[f], partner)

    def step(i, carry):
        @pl.when(i == 0)
        def _():
            wait(wbuf.at[0, 1 - h], wrecv.at[0])
            core_wait(z)

        @pl.when(i == 3)
        def _():
            wait(wbuf.at[1, 1 - h], wrecv.at[1])
            weight_send(2)

        @pl.when(i == 10)
        def _():
            wait(wbuf.at[2, 1 - h], wrecv.at[2])

        @pl.when((i == 1) | (i == 6) | (i == 15))
        def _():
            d = 1 + i // 6
            core_wait((z + d) % 8)
            core_wait((z + 8 - d) % 8)

        @pl.when(i == 17)
        def _():
            core_wait((z + 4) % 8)

        @pl.when(i < ITEMS)
        def _():
            forward(i)

        @pl.when(i <= 10)
        def _():
            tick(i + 3)

        @pl.when((i >= LAG_A) & (i < ITEMS + LAG_A))
        def _():
            terms(i - LAG_A)

        @pl.when(i >= LAG_B)
        def _():
            backward(i - LAG_B)

        done = i - LAG_B

        @pl.when((done >= 15) & (done % 3 == 2))
        def _():
            out_send((done - 15) // 3)
        return carry

    lax.fori_loop(0, ITEMS + LAG_B, step, 0)

    inverse = 1.0 / float(TOKENS)
    for f in range(NF):
        wait(orecv.at[f], orsem.at[f])
        cols = pl.ds(f * CHUNK, CHUNK)
        g = acc[f, h, :, pl.ds(0, CHUNK)] + orecv[f, :, pl.ds(0, CHUNK)].astype(jnp.float32)
        grad[:, cols] = (g * inverse).astype(jnp.bfloat16)
        e = acc[f, h, :, pl.ds(CHUNK, CHUNK)] + orecv[f, :, pl.ds(CHUNK, CHUNK)].astype(jnp.float32)
        probe = wbuf[f, h, :, pl.ds(CHUNK, CHUNK)].astype(jnp.float32)
        est[:, cols] = (probe * (e * inverse)).astype(jnp.bfloat16)

    for s in range(3):
        wait(region(z, c, 0), ysend.at[s])
    for way in range(2):
        wait(abuf.at[:, 0, pl.ds(0, 7), pl.ds(0, 128), :], zsend.at[way])
    wait(abuf.at[:, :, :, pl.ds(0, 128), :], csend)
    wait(wbuf.at[:, 0], wsend)
    wait(rbuf, rsend)
    wait(dbuf.at[:, :, pl.ds(0, 192), :], gsend)
    wait(osend, osem)


def per_device(*args):
    bf, f32 = jnp.bfloat16, jnp.float32
    dma = pltpu.SemaphoreType.DMA
    hidden = args[2].shape[1]
    return pl.pallas_call(
        kernel,
        out_shape=[jax.ShapeDtypeStruct((BLOCK, hidden), bf)] * 2,
        in_specs=[pl.BlockSpec(memory_space=pl.ANY)] * 5,
        out_specs=[pl.BlockSpec(memory_space=pltpu.VMEM)] * 2,
        scratch_shapes=[
            pltpu.VMEM((2, 2, 8, 256, BLOCK), bf),
            pltpu.VMEM((NF, 2, BLOCK, 3 * CHUNK), bf),
            pltpu.VMEM((NF, 8, 256, 3 * CHUNK), bf),
            pltpu.VMEM((4, 256, 3 * CHUNK), f32),
            pltpu.VMEM((NF, 8, 3, 64, 3 * CHUNK), bf),
            pltpu.VMEM((NF, 8, 256, 2 * CHUNK), bf),
            pltpu.VMEM((NF, 2, BLOCK, 2 * CHUNK), f32),
            pltpu.VMEM((NF, BLOCK, 2 * CHUNK), bf),
            pltpu.VMEM((NF, BLOCK, 2 * CHUNK), bf),
            dma, dma((NF,)),
            dma((3,)), dma((3,)),
            dma((2,)), dma((2, 14)),
            dma, dma((8,)),
            dma, dma((NF,)),
            dma, dma((NF, 8)),
            dma, dma((NF, 8)),
            dma, dma((NF,)),
        ],
        compiler_params=pltpu.CompilerParams(
            collective_id=0, has_side_effects=True, vmem_limit_bytes=56 * 2**20
        ),
        cost_estimate=pl.CostEstimate(flops=12 * 10**9, bytes_accessed=4 * 10**6, transcendentals=10**6),
    )(*args)


def solution(mesh):
    placed = (P("dp", "mp"), P("dp", "mp"), P("mp", "dp"), P("mp", "dp"), P("mp", "dp"))
    return jax.shard_map(
        per_device,
        mesh=mesh,
        in_specs=placed,
        out_specs=(P("mp", "dp"), P("mp", "dp")),
        check_vma=False,
    )
```

```python
import math

import jax
import jax.numpy as jnp
from jax import lax
from jax.experimental import pallas as pl
from jax.experimental.pallas import tpu as pltpu
from jax.sharding import PartitionSpec as P

MESH = pl.DeviceIdType.MESH
TOKENS = 4096
BLOCK = 768
CHUNK = 128
NF = 3
HALF = BLOCK // 2
ITEMS = 24
LAG_A, LAG_R, LAG_B = 2, 3, 5


def curvature_terms(preact, preact_dot, upstream):
    density = jnp.exp(-0.5 * preact * preact) / math.sqrt(2.0 * math.pi)
    cumulative = 0.5 * (1.0 + lax.erf(preact / math.sqrt(2.0)))
    slope = cumulative + preact * density
    bend = density * (2.0 - preact * preact)
    delta = (upstream * slope).astype(jnp.bfloat16)
    delta_dot = (upstream * bend * preact_dot).astype(jnp.bfloat16)
    return delta, delta_dot


def dot(a, b):
    return jnp.dot(a, b, preferred_element_type=jnp.float32)


def dot_t(a, b):
    return lax.dot_general(a, b, (((0,), (0,)), ((), ())), preferred_element_type=jnp.float32)


def item(i):
    f = jnp.where(i < 6, i // 3, jnp.where(i < 10, (i - 6) // 2, jnp.where(i < 15, 2, (i - 15) // 3)))
    j = jnp.where(i < 6, i % 3, jnp.where(i < 10, 3 + (i - 6) % 2, jnp.where(i < 15, i - 10, 5 + (i - 15) % 3)))
    return f, j


def kernel(normed, cotangent, up_weight, up_probe, down_weight, grad, est,
           abuf, wbuf, pbuf, ptmp, rbuf, dbuf, acc, osend, orecv, wpass,
           la, lw, ysend, yrecv, zsend, zrecv, csend, crecv, wsend, wrecv, wprecv,
           rsend, rrecv, gsend, grecv, hrecv, osem, orsem):
    dp, mp = lax.axis_index("dp"), lax.axis_index("mp")
    l, z, c = dp // 16, (dp // 2) % 8, dp % 2
    h, x = mp // 4, mp % 4

    def at(x_=x, h_=h, l_=l, z_=z, c_=c):
        return (l_ * 16 + z_ * 2 + c_, h_ * 4 + x_)

    def wait(ref, sem):
        pltpu.make_async_copy(ref, ref, sem).wait()

    def send(src, dst, ssem, rsem, device):
        pltpu.make_async_remote_copy(src_ref=src, dst_ref=dst, send_sem=ssem, recv_sem=rsem,
                                     device_id=device, device_id_type=MESH).start()

    x_peers = [at(x_=(x + dx) % 4) for dx in (1, 2, 3)]
    y_peers = [at(l_=1 - l), at(l_=1 - l, h_=1 - h), at(h_=1 - h)]
    z_peers = [at(z_=(z + 1) % 8), at(z_=(z + 7) % 8)]
    sibling = at(c_=1 - c)
    partner = at(h_=1 - h)

    def rows_of(cc, ll):
        return pl.ds(pl.multiple_of(cc * 128 + ll * 64, 64), 64)

    mine = pl.ds(pl.multiple_of(h * 64, 64), 64)
    theirs = pl.ds(pl.multiple_of((1 - h) * 64, 64), 64)
    inputs = (normed, cotangent)
    for n in range(2):
        pltpu.make_async_copy(inputs[n].at[mine, :], abuf.at[n, h, z, rows_of(c, l), :], la).start()
    for f in range(NF):
        for k, w in enumerate((up_weight, up_probe, down_weight)):
            pltpu.make_async_copy(w.at[:, pl.ds(f * CHUNK, CHUNK)],
                                  wbuf.at[f, h, :, pl.ds(k * CHUNK, CHUNK)], lw.at[f]).start()

    barrier = pltpu.get_barrier_semaphore()
    peers = x_peers + y_peers + z_peers + [sibling]
    for peer in peers:
        pl.semaphore_signal(barrier, inc=1, device_id=peer, device_id_type=MESH)
    pl.semaphore_wait(barrier, len(peers))

    def region(zz, cc, s):
        ll = (l + (s + 1) // 2) % 2
        hh = (h + s // 2) % 2
        return abuf.at[:, hh, zz, rows_of(cc, ll), :]

    def zpart(way, k):
        return (k % 4 + 2 * (k // 12)) % 4 if way else k % 4

    def ring_send(way, k):
        sign = -1 if way else 1
        zz = (z + 8 - sign * (k // 4)) % 8
        r = region(zz, c, zpart(way, k))
        send(r, r, zsend.at[way], zrecv.at[way, k], z_peers[way])

    def core_send(zz, s):
        r = region(zz, c, s)
        send(r, r, csend, crecv.at[zz], sibling)

    def core_wait(zz):
        wait(abuf.at[:, :, zz, pl.ds(pl.multiple_of((1 - c) * 128, 128), 128), :], crecv.at[zz])

    for s in (1, 2, 3):
        for n in range(2):
            send(inputs[n].at[mine if s == 1 else theirs, :], abuf.at[n, h, z, rows_of(c, l), :],
                 ysend.at[s - 1], yrecv.at[s - 1], y_peers[s - 1])

    def weight_send(f):
        wait(wbuf.at[f, h], lw.at[f])
        for way in range(2):
            send(wbuf.at[f, h, pl.ds(way * HALF, HALF), :], wpass.at[f, way],
                 wsend, wprecv.at[f, way], y_peers[way])

    def weight_forward(f):
        for way in range(2):
            wait(wpass.at[f, way], wprecv.at[f, way])
            send(wpass.at[f, way], wbuf.at[f, (h + way) % 2, pl.ds(way * HALF, HALF), :],
                 wsend, wrecv.at[f], y_peers[1 - way])

    wait(region(z, c, 0), la)
    ring_send(0, 0)
    ring_send(1, 0)
    core_send(z, 0)
    acc[...] = jnp.zeros_like(acc)
    for s in (1, 2, 3):
        if s == 3:
            weight_send(0)
        wait(region(z, c, s), yrecv.at[s - 1])
        ring_send(0, s)
        ring_send(1, s)
        core_send(z, s)

    def tick(k):
        for way in (0, 1):
            sign = -1 if way else 1
            zz = (z + 8 - sign * (k // 4 + 1)) % 8
            s = zpart(way, k)
            wait(region(zz, c, s), zrecv.at[way, k])
            if way == 0:
                @pl.when(k <= 9)
                def _():
                    ring_send(0, k + 4)
            else:
                @pl.when(k <= 7)
                def _():
                    ring_send(1, k + 4)

                @pl.when((k == 10) | (k == 11))
                def _():
                    ring_send(1, k + 2)
            core_send(zz, s)

    def early(k, carry):
        tick(k)

        @pl.when(k == 1)
        def _():
            weight_forward(0)
            weight_send(1)
        return carry

    lax.fori_loop(0, 3, early, 0)

    def packet(j):
        return (z + 8 + (2 * (j % 2) - 1) * ((j + 1) // 2)) % 8

    def x_rows(xx):
        return pl.ds(pl.multiple_of(xx * 64, 64), 64)

    def forward(i):
        f, j = item(i)
        zj = packet(j)
        slot = i % 4
        for n, cols in ((0, pl.ds(0, 2 * CHUNK)), (1, pl.ds(2 * CHUNK, CHUNK))):
            part = dot(abuf[n, 0, zj], wbuf[f, 0, :, cols]) + dot(abuf[n, 1, zj], wbuf[f, 1, :, cols])
            ptmp[slot, :, cols] = part
            pbuf[f, zj, :, cols] = part.astype(jnp.bfloat16)
        for dx in (1, 2, 3):
            send(pbuf.at[f, zj, x_rows((x + dx) % 4), :], rbuf.at[f, zj, dx - 1],
                 rsend, rrecv.at[f, zj], x_peers[dx - 1])

    def terms(i):
        f, j = item(i)
        zj = packet(j)
        slot = i % 4
        wait(rbuf.at[f, zj], rrecv.at[f, zj])

        def total(k):
            cols = pl.ds(k * CHUNK, CHUNK)
            t = ptmp[slot, x_rows(x), cols]
            for s in range(3):
                t = t + rbuf[f, zj, s, :, cols].astype(jnp.float32)
            return t

        delta, delta_dot = curvature_terms(total(0), total(1), total(2))
        dbuf[f, zj, x_rows(x), pl.ds(0, CHUNK)] = delta
        dbuf[f, zj, x_rows(x), pl.ds(CHUNK, CHUNK)] = delta_dot
        r = dbuf.at[f, zj, x_rows(x), :]
        for dx in (1, 3):
            send(r, r, gsend, grecv.at[f, zj], x_peers[dx - 1])

    def relay(i):
        f, j = item(i)
        zj = packet(j)
        wait(dbuf.at[f, zj, pl.ds(0, 128), :], grecv.at[f, zj])
        for dx, start in ((1, ((x + 3) % 4) * 64), (3, ((x + 1) % 4) * 64 + 32)):
            r = dbuf.at[f, zj, pl.ds(pl.multiple_of(start, 32), 32), :]
            send(r, r, gsend, hrecv.at[f, zj], x_peers[dx - 1])

    def backward(i):
        f, j = item(i)
        zj = packet(j)
        wait(dbuf.at[f, zj, pl.ds(0, 64), :], hrecv.at[f, zj])
        d = dbuf[f, zj]
        for hh in range(2):
            acc[f, hh] += dot_t(abuf[0, hh, zj], d)

    def out_send(f):
        osend[f] = acc[f, 1 - h].astype(jnp.bfloat16)
        send(osend.at[f], orecv.at[f], osem, orsem.at[f], partner)

    def step(i, carry):
        @pl.when(i == 0)
        def _():
            wait(wbuf.at[0, 1 - h], wrecv.at[0])
            core_wait(z)

        @pl.when(i == 3)
        def _():
            wait(wbuf.at[1, 1 - h], wrecv.at[1])

        @pl.when(i == 10)
        def _():
            wait(wbuf.at[2, 1 - h], wrecv.at[2])

        @pl.when((i == 1) | (i == 6) | (i == 15))
        def _():
            d = 1 + i // 6
            core_wait((z + d) % 8)
            core_wait((z + 8 - d) % 8)

        @pl.when(i == 17)
        def _():
            core_wait((z + 4) % 8)

        @pl.when(i < ITEMS)
        def _():
            forward(i)

        @pl.when(i <= 10)
        def _():
            tick(i + 3)

        @pl.when(i == 0)
        def _():
            weight_forward(1)
            weight_send(2)

        @pl.when(i == 3)
        def _():
            weight_forward(2)

        @pl.when((i >= LAG_A) & (i < ITEMS + LAG_A))
        def _():
            terms(i - LAG_A)

        @pl.when((i >= LAG_R) & (i < ITEMS + LAG_R))
        def _():
            relay(i - LAG_R)

        @pl.when(i >= LAG_B)
        def _():
            backward(i - LAG_B)

        done = i - LAG_B

        @pl.when((done >= 15) & (done % 3 == 2))
        def _():
            out_send((done - 15) // 3)
        return carry

    lax.fori_loop(0, ITEMS + LAG_B, step, 0)

    inverse = 1.0 / float(TOKENS)
    for f in range(NF):
        wait(orecv.at[f], orsem.at[f])
        cols = pl.ds(f * CHUNK, CHUNK)
        g = acc[f, h, :, pl.ds(0, CHUNK)] + orecv[f, :, pl.ds(0, CHUNK)].astype(jnp.float32)
        grad[:, cols] = (g * inverse).astype(jnp.bfloat16)
        e = acc[f, h, :, pl.ds(CHUNK, CHUNK)] + orecv[f, :, pl.ds(CHUNK, CHUNK)].astype(jnp.float32)
        probe = wbuf[f, h, :, pl.ds(CHUNK, CHUNK)].astype(jnp.float32)
        est[:, cols] = (probe * (e * inverse)).astype(jnp.bfloat16)

    for s in range(3):
        wait(region(z, c, 0), ysend.at[s])
    for way in range(2):
        wait(abuf.at[:, 0, pl.ds(0, 7), pl.ds(0, 128), :], zsend.at[way])
    wait(abuf.at[:, :, :, pl.ds(0, 128), :], csend)
    wait(wbuf, wsend)
    wait(rbuf, rsend)
    wait(dbuf.at[:, :, pl.ds(0, 192), :], gsend)
    wait(osend, osem)


def per_device(*args):
    bf, f32 = jnp.bfloat16, jnp.float32
    dma = pltpu.SemaphoreType.DMA
    hidden = args[2].shape[1]
    return pl.pallas_call(
        kernel,
        out_shape=[jax.ShapeDtypeStruct((BLOCK, hidden), bf)] * 2,
        in_specs=[pl.BlockSpec(memory_space=pl.ANY)] * 5,
        out_specs=[pl.BlockSpec(memory_space=pltpu.VMEM)] * 2,
        scratch_shapes=[
            pltpu.VMEM((2, 2, 8, 256, BLOCK), bf),
            pltpu.VMEM((NF, 2, BLOCK, 3 * CHUNK), bf),
            pltpu.VMEM((NF, 8, 256, 3 * CHUNK), bf),
            pltpu.VMEM((4, 256, 3 * CHUNK), f32),
            pltpu.VMEM((NF, 8, 3, 64, 3 * CHUNK), bf),
            pltpu.VMEM((NF, 8, 256, 2 * CHUNK), bf),
            pltpu.VMEM((NF, 2, BLOCK, 2 * CHUNK), f32),
            pltpu.VMEM((NF, BLOCK, 2 * CHUNK), bf),
            pltpu.VMEM((NF, BLOCK, 2 * CHUNK), bf),
            pltpu.VMEM((NF, 2, HALF, 3 * CHUNK), bf),
            dma, dma((NF,)),
            dma((3,)), dma((3,)),
            dma((2,)), dma((2, 14)),
            dma, dma((8,)),
            dma, dma((NF,)), dma((NF, 2)),
            dma, dma((NF, 8)),
            dma, dma((NF, 8)), dma((NF, 8)),
            dma, dma((NF,)),
        ],
        compiler_params=pltpu.CompilerParams(
            collective_id=0, has_side_effects=True, vmem_limit_bytes=56 * 2**20
        ),
        cost_estimate=pl.CostEstimate(flops=12 * 10**9, bytes_accessed=4 * 10**6, transcendentals=10**6),
    )(*args)


def solution(mesh):
    placed = (P("dp", "mp"), P("dp", "mp"), P("mp", "dp"), P("mp", "dp"), P("mp", "dp"))
    return jax.shard_map(
        per_device,
        mesh=mesh,
        in_specs=placed,
        out_specs=(P("mp", "dp"), P("mp", "dp")),
        check_vma=False,
    )
```

```python
import math

import jax
import jax.numpy as jnp
from jax import lax
from jax.experimental import pallas as pl
from jax.experimental.pallas import tpu as pltpu
from jax.sharding import PartitionSpec as P

MESH = pl.DeviceIdType.MESH
TOKENS = 4096
BLOCK = 768
CHUNK = 128
NF = 3
HALF = BLOCK // 2
ITEMS = 24
LAG_A, LAG_R, LAG_B = 2, 3, 5


def curvature_terms(preact, preact_dot, upstream):
    density = jnp.exp(-0.5 * preact * preact) / math.sqrt(2.0 * math.pi)
    cumulative = 0.5 * (1.0 + lax.erf(preact / math.sqrt(2.0)))
    slope = cumulative + preact * density
    bend = density * (2.0 - preact * preact)
    delta = (upstream * slope).astype(jnp.bfloat16)
    delta_dot = (upstream * bend * preact_dot).astype(jnp.bfloat16)
    return delta, delta_dot


def dot(a, b):
    return jnp.dot(a, b, preferred_element_type=jnp.float32)


def dot_t(a, b):
    return lax.dot_general(a, b, (((0,), (0,)), ((), ())), preferred_element_type=jnp.float32)


def item(i):
    f = jnp.where(i < 6, i // 3, jnp.where(i < 10, (i - 6) // 2, jnp.where(i < 15, 2, (i - 15) // 3)))
    j = jnp.where(i < 6, i % 3, jnp.where(i < 10, 3 + (i - 6) % 2, jnp.where(i < 15, i - 10, 5 + (i - 15) % 3)))
    return f, j


def kernel(normed, cotangent, up_weight, up_probe, down_weight, grad, est,
           abuf, wbuf, pbuf, ptmp, rbuf, dbuf, acc, osend, orecv, wpass,
           la, lw, ysend, yrecv, zsend, zrecv, csend, crecv, wsend, wrecv, wprecv,
           rsend, rrecv, gsend, grecv, hrecv, osem, orsem):
    dp, mp = lax.axis_index("dp"), lax.axis_index("mp")
    l, z, c = dp // 16, (dp // 2) % 8, dp % 2
    h, x = mp // 4, mp % 4

    def at(x_=x, h_=h, l_=l, z_=z, c_=c):
        return (l_ * 16 + z_ * 2 + c_, h_ * 4 + x_)

    def wait(ref, sem):
        pltpu.make_async_copy(ref, ref, sem).wait()

    def send(src, dst, ssem, rsem, device):
        pltpu.make_async_remote_copy(src_ref=src, dst_ref=dst, send_sem=ssem, recv_sem=rsem,
                                     device_id=device, device_id_type=MESH).start()

    x_peers = [at(x_=(x + dx) % 4) for dx in (1, 2, 3)]
    y_peers = [at(l_=1 - l), at(l_=1 - l, h_=1 - h), at(h_=1 - h)]
    z_peers = [at(z_=(z + 1) % 8), at(z_=(z + 7) % 8)]
    sibling = at(c_=1 - c)
    partner = at(h_=1 - h)

    def rows_of(cc, ll):
        return pl.ds(pl.multiple_of(cc * 128 + ll * 64, 64), 64)

    mine = pl.ds(pl.multiple_of(h * 64, 64), 64)
    theirs = pl.ds(pl.multiple_of((1 - h) * 64, 64), 64)
    inputs = (normed, cotangent)
    for n in range(2):
        pltpu.make_async_copy(inputs[n].at[mine, :], abuf.at[n, h, z, rows_of(c, l), :], la).start()
    for f in range(NF):
        for k, w in enumerate((up_weight, up_probe, down_weight)):
            pltpu.make_async_copy(w.at[:, pl.ds(f * CHUNK, CHUNK)],
                                  wbuf.at[f, h, :, pl.ds(k * CHUNK, CHUNK)], lw.at[f]).start()

    barrier = pltpu.get_barrier_semaphore()
    peers = x_peers + y_peers + z_peers + [sibling]
    for peer in peers:
        pl.semaphore_signal(barrier, inc=1, device_id=peer, device_id_type=MESH)
    pl.semaphore_wait(barrier, len(peers))

    def region(zz, cc, s):
        ll = (l + (s + 1) // 2) % 2
        hh = (h + s // 2) % 2
        return abuf.at[:, hh, zz, rows_of(cc, ll), :]

    def zpart(way, k):
        return (k % 4 + 2 * (k // 12)) % 4 if way else k % 4

    def ring_send(way, k):
        sign = -1 if way else 1
        zz = (z + 8 - sign * (k // 4)) % 8
        r = region(zz, c, zpart(way, k))
        send(r, r, zsend.at[way], zrecv.at[way, k], z_peers[way])

    def core_send(zz, s):
        r = region(zz, c, s)
        send(r, r, csend, crecv.at[zz], sibling)

    def core_wait(zz):
        wait(abuf.at[:, :, zz, pl.ds(pl.multiple_of((1 - c) * 128, 128), 128), :], crecv.at[zz])

    for s in (1, 2, 3):
        for n in range(2):
            send(inputs[n].at[mine if s == 1 else theirs, :], abuf.at[n, h, z, rows_of(c, l), :],
                 ysend.at[s - 1], yrecv.at[s - 1], y_peers[s - 1])

    def weight_send(f):
        wait(wbuf.at[f, h], lw.at[f])
        for way in range(2):
            send(wbuf.at[f, h, pl.ds(way * HALF, HALF), :], wpass.at[f, way],
                 wsend, wprecv.at[f, way], y_peers[way])

    def weight_forward(f):
        for way in range(2):
            wait(wpass.at[f, way], wprecv.at[f, way])
            send(wpass.at[f, way], wbuf.at[f, (h + way) % 2, pl.ds(way * HALF, HALF), :],
                 wsend, wrecv.at[f], y_peers[1 - way])

    wait(region(z, c, 0), la)
    ring_send(0, 0)
    ring_send(1, 0)
    core_send(z, 0)
    acc[...] = jnp.zeros_like(acc)
    for s in (1, 2, 3):
        if s == 3:
            weight_send(0)
        wait(region(z, c, s), yrecv.at[s - 1])
        ring_send(0, s)
        ring_send(1, s)
        core_send(z, s)

    def tick(k):
        for way in (0, 1):
            sign = -1 if way else 1
            zz = (z + 8 - sign * (k // 4 + 1)) % 8
            s = zpart(way, k)
            wait(region(zz, c, s), zrecv.at[way, k])
            if way == 0:
                @pl.when(k <= 9)
                def _():
                    ring_send(0, k + 4)
            else:
                @pl.when(k <= 7)
                def _():
                    ring_send(1, k + 4)

                @pl.when((k == 10) | (k == 11))
                def _():
                    ring_send(1, k + 2)
            core_send(zz, s)

    def early(k, carry):
        tick(k)

        @pl.when(k == 1)
        def _():
            weight_forward(0)
            weight_send(1)
        return carry

    lax.fori_loop(0, 4, early, 0)

    def packet(j):
        return (z + 8 + (2 * (j % 2) - 1) * ((j + 1) // 2)) % 8

    def x_rows(xx):
        return pl.ds(pl.multiple_of(xx * 64, 64), 64)

    def forward(i):
        f, j = item(i)
        zj = packet(j)
        slot = i % 4
        for n, cols in ((0, pl.ds(0, 2 * CHUNK)), (1, pl.ds(2 * CHUNK, CHUNK))):
            part = dot(abuf[n, 0, zj], wbuf[f, 0, :, cols]) + dot(abuf[n, 1, zj], wbuf[f, 1, :, cols])
            ptmp[slot, :, cols] = part
            pbuf[f, zj, :, cols] = part.astype(jnp.bfloat16)
        for dx in (1, 2, 3):
            send(pbuf.at[f, zj, x_rows((x + dx) % 4), :], rbuf.at[f, zj, dx - 1],
                 rsend, rrecv.at[f, zj], x_peers[dx - 1])

    def terms(i):
        f, j = item(i)
        zj = packet(j)
        slot = i % 4
        wait(rbuf.at[f, zj], rrecv.at[f, zj])

        def total(k):
            cols = pl.ds(k * CHUNK, CHUNK)
            t = ptmp[slot, x_rows(x), cols]
            for s in range(3):
                t = t + rbuf[f, zj, s, :, cols].astype(jnp.float32)
            return t

        delta, delta_dot = curvature_terms(total(0), total(1), total(2))
        dbuf[f, zj, x_rows(x), pl.ds(0, CHUNK)] = delta
        dbuf[f, zj, x_rows(x), pl.ds(CHUNK, CHUNK)] = delta_dot
        r = dbuf.at[f, zj, x_rows(x), :]
        for dx in (1, 3):
            send(r, r, gsend, grecv.at[f, zj], x_peers[dx - 1])

    def relay(i):
        f, j = item(i)
        zj = packet(j)
        wait(dbuf.at[f, zj, pl.ds(0, 128), :], grecv.at[f, zj])
        for dx, start in ((1, ((x + 3) % 4) * 64), (3, ((x + 1) % 4) * 64 + 32)):
            r = dbuf.at[f, zj, pl.ds(pl.multiple_of(start, 32), 32), :]
            send(r, r, gsend, hrecv.at[f, zj], x_peers[dx - 1])

    def backward(i):
        f, j = item(i)
        zj = packet(j)
        wait(dbuf.at[f, zj, pl.ds(0, 64), :], hrecv.at[f, zj])
        d = dbuf[f, zj]
        for hh in range(2):
            acc[f, hh] += dot_t(abuf[0, hh, zj], d)

    def out_send(f):
        osend[f] = acc[f, 1 - h].astype(jnp.bfloat16)
        send(osend.at[f], orecv.at[f], osem, orsem.at[f], partner)

    def step(i, carry):
        @pl.when(i == 0)
        def _():
            wait(wbuf.at[0, 1 - h], wrecv.at[0])
            core_wait(z)

        @pl.when(i == 3)
        def _():
            wait(wbuf.at[1, 1 - h], wrecv.at[1])

        @pl.when(i == 10)
        def _():
            wait(wbuf.at[2, 1 - h], wrecv.at[2])

        @pl.when((i == 1) | (i == 6) | (i == 15))
        def _():
            d = 1 + i // 6
            core_wait((z + d) % 8)
            core_wait((z + 8 - d) % 8)

        @pl.when(i == 17)
        def _():
            core_wait((z + 4) % 8)

        @pl.when(i < ITEMS)
        def _():
            forward(i)

        @pl.when((i < 14) & (i % 3 != 2))
        def _():
            tick(4 + (2 * i + 2) // 3)

        @pl.when(i == 0)
        def _():
            weight_forward(1)
            weight_send(2)

        @pl.when(i == 3)
        def _():
            weight_forward(2)

        @pl.when((i >= LAG_A) & (i < ITEMS + LAG_A))
        def _():
            terms(i - LAG_A)

        @pl.when((i >= LAG_R) & (i < ITEMS + LAG_R))
        def _():
            relay(i - LAG_R)

        @pl.when(i >= LAG_B)
        def _():
            backward(i - LAG_B)

        done = i - LAG_B

        @pl.when((done >= 15) & (done % 3 == 2))
        def _():
            out_send((done - 15) // 3)
        return carry

    lax.fori_loop(0, ITEMS + LAG_B, step, 0)

    inverse = 1.0 / float(TOKENS)
    for f in range(NF):
        wait(orecv.at[f], orsem.at[f])
        cols = pl.ds(f * CHUNK, CHUNK)
        g = acc[f, h, :, pl.ds(0, CHUNK)] + orecv[f, :, pl.ds(0, CHUNK)].astype(jnp.float32)
        grad[:, cols] = (g * inverse).astype(jnp.bfloat16)
        e = acc[f, h, :, pl.ds(CHUNK, CHUNK)] + orecv[f, :, pl.ds(CHUNK, CHUNK)].astype(jnp.float32)
        probe = wbuf[f, h, :, pl.ds(CHUNK, CHUNK)].astype(jnp.float32)
        est[:, cols] = (probe * (e * inverse)).astype(jnp.bfloat16)

    for s in range(3):
        wait(region(z, c, 0), ysend.at[s])
    for way in range(2):
        wait(abuf.at[:, 0, pl.ds(0, 7), pl.ds(0, 128), :], zsend.at[way])
    wait(abuf.at[:, :, :, pl.ds(0, 128), :], csend)
    wait(wbuf, wsend)
    wait(rbuf, rsend)
    wait(dbuf.at[:, :, pl.ds(0, 192), :], gsend)
    wait(osend, osem)


def per_device(*args):
    bf, f32 = jnp.bfloat16, jnp.float32
    dma = pltpu.SemaphoreType.DMA
    hidden = args[2].shape[1]
    return pl.pallas_call(
        kernel,
        out_shape=[jax.ShapeDtypeStruct((BLOCK, hidden), bf)] * 2,
        in_specs=[pl.BlockSpec(memory_space=pl.ANY)] * 5,
        out_specs=[pl.BlockSpec(memory_space=pltpu.VMEM)] * 2,
        scratch_shapes=[
            pltpu.VMEM((2, 2, 8, 256, BLOCK), bf),
            pltpu.VMEM((NF, 2, BLOCK, 3 * CHUNK), bf),
            pltpu.VMEM((NF, 8, 256, 3 * CHUNK), bf),
            pltpu.VMEM((4, 256, 3 * CHUNK), f32),
            pltpu.VMEM((NF, 8, 3, 64, 3 * CHUNK), bf),
            pltpu.VMEM((NF, 8, 256, 2 * CHUNK), bf),
            pltpu.VMEM((NF, 2, BLOCK, 2 * CHUNK), f32),
            pltpu.VMEM((NF, BLOCK, 2 * CHUNK), bf),
            pltpu.VMEM((NF, BLOCK, 2 * CHUNK), bf),
            pltpu.VMEM((NF, 2, HALF, 3 * CHUNK), bf),
            dma, dma((NF,)),
            dma((3,)), dma((3,)),
            dma((2,)), dma((2, 14)),
            dma, dma((8,)),
            dma, dma((NF,)), dma((NF, 2)),
            dma, dma((NF, 8)),
            dma, dma((NF, 8)), dma((NF, 8)),
            dma, dma((NF,)),
        ],
        compiler_params=pltpu.CompilerParams(
            collective_id=0, has_side_effects=True, vmem_limit_bytes=56 * 2**20
        ),
        cost_estimate=pl.CostEstimate(flops=12 * 10**9, bytes_accessed=4 * 10**6, transcendentals=10**6),
    )(*args)


def solution(mesh):
    placed = (P("dp", "mp"), P("dp", "mp"), P("mp", "dp"), P("mp", "dp"), P("mp", "dp"))
    return jax.shard_map(
        per_device,
        mesh=mesh,
        in_specs=placed,
        out_specs=(P("mp", "dp"), P("mp", "dp")),
        check_vma=False,
    )
```
